256 devices in a mesh: band: 4 (over z_hi), slab: 64 (over y, x, z_lo, core).
Axes of the slice: x: 4, y: 4, z: 8 (z_hi: 4, z_lo: 2; z = z_hi * 2 + z_lo), core: 2. Of those that a mesh axis runs over, the one named last changes fastest.
Arguments:
- orbitals: float32 [2, 64, 128, 128, 128], P(None, 'band', 'slab'), may hold values from -6 to 6
- occupations: float32 [64], P('band'), may hold values from 0.01 to 0.1
- rest_density: float32 [128, 128, 128], P('slab'), may hold values from 1 to 8
- ionic_potential: float32 [128, 128, 128], P('slab'), may hold values from -6 to 6
Outputs:
- taylor_term: float32 [2, 64, 128, 128, 128], P(None, 'band', 'slab')
- potential: float32 [128, 128, 128], P('slab')
The draws below stay inside these ranges and needn't reach their ends.
All inputs are finite; a program needn't handle non-finite values.
Results may differ from the reference program's by a relative error of at most 0.0003.
Values sent between devices are 32-bit elements; how exact they have to be, the bound alone decides.
A program may use at most 64 MiB of HBM per device.

```python
import math
import jax
import jax.numpy as jnp
from jax import lax

NG = 128
ORBS = 64


def steps_of(rng, dims, shards, smallest, largest):
    loudness, own = 1.0, jax.random.fold_in(rng, 6)
    for position, parts in shards:
        draws = jnp.exp(jax.random.uniform(jax.random.fold_in(own, position), (parts,), jnp.float32, smallest / len(shards), largest / len(shards)))
        loudness = loudness * jnp.repeat(draws, dims[position] // parts).reshape([-1 if axis == position else 1 for axis in range(len(dims))])
    return loudness


def scatter_about(own_key, extent, width, bound, pieces=(), kind=jnp.bfloat16):
    loudness = steps_of(own_key, extent, pieces, -0.22, 0.18) if pieces else 1.0
    values = jax.random.normal(own_key, extent, jnp.float32) * width * loudness
    return jnp.minimum(jnp.maximum(values, -bound), bound).astype(kind)


def setup_inputs(seed: int = 0) -> dict:
    seeds = jax.random.split(jax.random.key(seed), 5)
    orbitals = scatter_about(seeds[0], (2, ORBS, NG, NG, NG), 1.0, 6.0, ((1, 4), (2, 64)), jnp.float32)
    occupations = jnp.clip(jnp.exp(math.log(0.1) - 2.3025851 * jax.random.uniform(seeds[1], (ORBS,), jnp.float32) ** steps_of(seeds[1], (ORBS,), ((0, 4),), -0.2, 0.2)), 0.01, 0.1)
    rest_density = jnp.clip(jnp.exp(math.log(8.0) - 2.0794415 * jax.random.uniform(seeds[2], (NG, NG, NG), jnp.float32) ** steps_of(seeds[2], (NG, NG, NG), ((0, 64),), -0.2, 0.2)), 1.0, 8.0)
    ionic_potential = scatter_about(seeds[3], (NG, NG, NG), 1.0, 6.0, ((0, 64),), jnp.float32)
    return {"orbitals": orbitals, "occupations": occupations, "rest_density": rest_density, "ionic_potential": ionic_potential}


grid_spacing = 0.4
time_step = 0.01
exchange_factor = (3.0 / math.pi) ** (1.0 / 3.0)


def wavenumbers(points):
    indices = jnp.arange(points, dtype=jnp.int32)
    signed = jnp.where(indices < points // 2, indices, indices - points)
    return (2.0 * math.pi / (points * grid_spacing)) * signed.astype(jnp.float32)


def reference(orbitals, occupations, rest_density, ionic_potential):
    axis_waves = wavenumbers(NG)
    squared = axis_waves * axis_waves
    grid_g2 = squared[:, None, None] + squared[None, :, None] + squared[None, None, :]
    positive = grid_g2 > 0
    green = jnp.where(positive, 4.0 * math.pi / jnp.where(positive, grid_g2, 1.0), 0.0)

    def accumulate(running, entries):
        weight, real_part, imag_part = entries
        return running + weight * (real_part * real_part + imag_part * imag_part), None

    partial_sum, unused = lax.scan(accumulate, jnp.zeros_like(rest_density), (occupations, orbitals[0], orbitals[1]))
    density = rest_density + partial_sum
    hartree = jnp.real(jnp.fft.ifftn(green * jnp.fft.fftn(density))).astype(rest_density.dtype)
    exchange_xc = -exchange_factor * jnp.cbrt(density)
    potential = ionic_potential + hartree + exchange_xc

    def apply_one(pair):
        psi = pair[0] + 1j * pair[1]
        kinetic = jnp.fft.ifftn(0.5 * grid_g2 * jnp.fft.fftn(psi))
        applied = kinetic + potential * psi
        return jnp.stack([time_step * jnp.imag(applied), -time_step * jnp.real(applied)]).astype(orbitals.dtype)

    terms = lax.map(apply_one, jnp.swapaxes(orbitals, 0, 1))
    return jnp.swapaxes(terms, 0, 1), potential
```

```python
import math

import jax
import jax.numpy as jnp
import numpy as np
from jax import lax
from jax.sharding import PartitionSpec as P

grid_spacing = 0.4
time_step = 0.01
exchange_factor = (3.0 / math.pi) ** (1.0 / 3.0)


def wavenumbers_squared(points):
    indices = np.arange(points)
    signed = np.where(indices < points // 2, indices, indices - points)
    return (2.0 * math.pi / (points * grid_spacing) * signed) ** 2


def real_basis(points):
    j = np.arange(points)[:, None]
    x = np.arange(points)[None, :]
    cosine = np.cos(2.0 * math.pi * (j * x % points) / points)
    sine = np.sin(2.0 * math.pi * ((points - j) * x % points) / points)
    rows = np.where(j <= points // 2, cosine, sine) * math.sqrt(2.0 / points)
    return np.where((j == 0) | (j == points // 2), rows * math.sqrt(0.5), rows)


def local(orbitals, occupations, rest_density, ionic_potential):
    points = orbitals.shape[3]
    pencil_rows = points // lax.axis_size("slab")
    basis64 = real_basis(points)
    squared64 = wavenumbers_squared(points)
    basis = jnp.asarray(basis64, jnp.float32)
    kinetic = jnp.asarray(basis64.T @ (0.5 * squared64[:, None] * basis64), jnp.float32)
    squared = jnp.asarray(squared64, jnp.float32)

    def product(spec, a, b):
        return jnp.einsum(spec, a, b, precision=lax.Precision.HIGHEST)

    pencil = lax.all_to_all(orbitals, "slab", split_axis=3, concat_axis=2, tiled=True)
    first_back = lax.all_to_all(
        product("poxyz,xk->pokyz", pencil, kinetic), "slab", split_axis=2, concat_axis=3, tiled=True
    )

    squares = orbitals[0] * orbitals[0] + orbitals[1] * orbitals[1]
    partial_sum = jnp.sum(occupations[:, None, None, None] * squares, axis=0)
    density = rest_density + lax.psum(partial_sum, "band")
    exchange_xc = -exchange_factor * jnp.cbrt(density)
    spectrum = product("xkz,jk->xjz", product("xyz,kz->xyk", density, basis), basis)
    spectrum = lax.all_to_all(spectrum, "slab", split_axis=1, concat_axis=0, tiled=True)
    own_squared = lax.dynamic_slice(squared, (lax.axis_index("slab") * pencil_rows,), (pencil_rows,))
    g2 = squared[:, None, None] + own_squared[None, :, None] + squared[None, None, :]
    positive = g2 > 0
    green = jnp.where(positive, 4.0 * math.pi / jnp.where(positive, g2, 1.0), 0.0)
    lines = product("xyz,kx->kyz", spectrum, basis) * green
    lines = product("kyz,kx->xyz", lines, basis)
    back = lax.all_to_all(lines, "slab", split_axis=0, concat_axis=1, tiled=True)
    hartree = product("xkz,ky->xyz", product("xyk,kz->xyz", back, basis), basis)
    potential = ionic_potential + hartree + exchange_xc

    planes = product("poxyz,yk->poxkz", orbitals, kinetic) + product("poxyz,zk->poxyk", orbitals, kinetic)
    applied = first_back + planes + potential * orbitals
    taylor_term = jnp.stack([time_step * applied[1], -time_step * applied[0]])
    return (taylor_term, potential)


def solution(mesh):
    return jax.shard_map(
        local,
        mesh=mesh,
        in_specs=(
            P(None, "band", "slab", None, None),
            P("band"),
            P("slab", None, None),
            P("slab", None, None),
        ),
        out_specs=(P(None, "band", "slab", None, None), P("slab", None, None)),
        check_vma=False,
    )
```

```python
import functools
import math

import jax
import jax.numpy as jnp
import numpy as np
from jax import lax
from jax.experimental import pallas as pl
from jax.experimental.pallas import tpu as pltpu
from jax.sharding import PartitionSpec as P

MESH = pl.DeviceIdType.MESH
grid_spacing = 0.4
time_step = 0.01
exchange_factor = (3.0 / math.pi) ** (1.0 / 3.0)
CHUNKS = 4


def wavenumbers_squared(points):
    indices = np.arange(points)
    signed = np.where(indices < points // 2, indices, indices - points)
    return (2.0 * math.pi / (points * grid_spacing) * signed) ** 2


def real_basis(points):
    j = np.arange(points)[:, None]
    x = np.arange(points)[None, :]
    cosine = np.cos(2.0 * math.pi * (j * x % points) / points)
    sine = np.sin(2.0 * math.pi * ((points - j) * x % points) / points)
    rows = np.where(j <= points // 2, cosine, sine) * math.sqrt(2.0 / points)
    return np.where((j == 0) | (j == points // 2), rows * math.sqrt(0.5), rows)


def kinetic_matrix(points):
    basis = real_basis(points)
    return basis.T @ (0.5 * wavenumbers_squared(points)[:, None] * basis)


def split(values):
    high = values.astype(jnp.bfloat16)
    return high, (values - high.astype(jnp.float32)).astype(jnp.bfloat16)


def dot(a, b):
    return jnp.dot(a, b, preferred_element_type=jnp.float32)


def left(matrix_high, matrix_low, values):
    high, low = split(values)
    return dot(jnp.concatenate([matrix_high, matrix_high], 1), jnp.concatenate([high, low], 0)) + dot(matrix_low, high)


def right(values, matrix_high, matrix_low):
    high, low = split(values)
    return dot(jnp.concatenate([high, low], 1), jnp.concatenate([matrix_high, matrix_high], 0)) + dot(high, matrix_low)


def partner(me, step):
    step = lax.rem(step * 37, 64)
    y = lax.rem(me // 16 + step // 16, 4)
    x = lax.rem(lax.rem(me // 4, 4) + lax.rem(step // 4, 4), 4)
    return y * 16 + x * 4 + jnp.bitwise_xor(lax.rem(me, 4), lax.rem(step, 4))


def kernel(
    high_ref, low_ref, psi_hbm, out_hbm,
    psi, pen, res, back, acc,
    load_sem, out_sem, self_sem, fwd_send, fwd_recv, bwd_send, bwd_recv,
):
    band, me = lax.axis_index("band"), lax.axis_index("slab")
    load = pltpu.make_async_copy(psi_hbm, psi, load_sem)
    load.start()
    barrier = pltpu.get_barrier_semaphore()

    @pl.loop(1, 64)
    def _(step):
        pl.semaphore_signal(barrier, inc=1, device_id=(band, partner(me, step)), device_id_type=MESH)

    load.wait()
    pl.semaphore_wait(barrier, 63)

    def field_part(ref, owner, c):
        rows = pl.ds(pl.multiple_of(owner // 4 * 8, 8), 8)
        return ref.at[:, lax.rem(owner, 4) * 4 + c, :, rows, :]

    def forward(c):
        @pl.loop(1, 64)
        def _(step):
            other = partner(me, step)
            pltpu.make_async_remote_copy(
                src_ref=field_part(psi, other, c), dst_ref=pen.at[c, :, me],
                send_sem=fwd_send.at[c], recv_sem=fwd_recv.at[c],
                device_id=(band, other), device_id_type=MESH,
            ).start()

        pltpu.make_async_copy(field_part(psi, me, c), pen.at[c, :, me], self_sem.at[0, c]).start()

    def backward(c):
        @pl.loop(1, 64)
        def _(step):
            other = partner(me, step)
            pltpu.make_async_remote_copy(
                src_ref=res.at[c, :, other], dst_ref=field_part(back, me, c),
                send_sem=bwd_send.at[c], recv_sem=bwd_recv.at[c],
                device_id=(band, other), device_id_type=MESH,
            ).start()

        pltpu.make_async_copy(res.at[c, :, me], field_part(back, me, c), self_sem.at[1, c]).start()

    def wait_all(sem):
        part = pen.at[0, :, pl.ds(0, 63)]
        pltpu.make_async_copy(part, part, sem).wait()

    def wait_one(sem):
        part = pen.at[0, :, 0]
        pltpu.make_async_copy(part, part, sem).wait()

    def lines(c):
        wait_all(fwd_recv.at[c])
        wait_one(self_sem.at[0, c])
        source, target = pen.reshape(CHUNKS, 2, 1024, 128), res.reshape(CHUNKS, 2, 1024, 128)
        for row in range(8):
            rows = pl.ds(row, 128, stride=8)
            values = jnp.concatenate([source[c, 0, rows, :], source[c, 1, rows, :]], 1)
            values = left(high_ref[...], low_ref[...], values)
            target[c, 0, rows, :] = values[:, :128]
            target[c, 1, rows, :] = values[:, 128:]

    def planes(c):
        @pl.loop(0, 8)
        def _(i):
            o, x = i // 2 * 4 + c, lax.rem(i, 2)
            real, imag = psi[0, o, x], psi[1, o, x]
            along_y = left(high_ref[...], low_ref[...], jnp.concatenate([real, imag], 1))
            along_z = right(jnp.concatenate([real, imag], 0), high_ref[...], low_ref[...])
            acc[0, o, x] = along_y[:, :128] + along_z[:128]
            acc[1, o, x] = along_y[:, 128:] + along_z[128:]

    def finish(c):
        wait_all(bwd_recv.at[c])
        wait_one(self_sem.at[1, c])

        @pl.loop(0, 4)
        def _(group):
            o = group * 4 + c
            acc[:, o] = acc[:, o] + back[:, o]
            pltpu.make_async_copy(acc.at[:, o], out_hbm.at[:, o], out_sem).start()

    for c in range(CHUNKS):
        forward(c)
    for c in range(CHUNKS):
        planes(c)
        lines(c)
        backward(c)
    for c in range(CHUNKS):
        finish(c)
    for c in range(CHUNKS):
        wait_all(fwd_send.at[c])
        wait_all(bwd_send.at[c])
    pltpu.make_async_copy(acc, out_hbm, out_sem).wait()


def kinetic(orbitals):
    points = orbitals.shape[3]
    matrix = jnp.asarray(kinetic_matrix(points), jnp.float32)
    high, low = split(matrix)
    field = pltpu.VMEM(orbitals.shape, jnp.float32)
    pencil = pltpu.VMEM((CHUNKS, 2, 64, 2, 8, points), jnp.float32)
    dma = pltpu.SemaphoreType.DMA
    return pl.pallas_call(
        kernel,
        out_shape=jax.ShapeDtypeStruct(orbitals.shape, jnp.float32),
        in_specs=[pl.BlockSpec(memory_space=pltpu.VMEM)] * 2 + [pl.BlockSpec(memory_space=pl.ANY)],
        out_specs=pl.BlockSpec(memory_space=pl.ANY),
        scratch_shapes=[
            field, pencil, pencil, field, field,
            dma, dma, dma((2, CHUNKS)), dma((CHUNKS,)), dma((CHUNKS,)), dma((CHUNKS,)), dma((CHUNKS,)),
        ],
        compiler_params=pltpu.CompilerParams(collective_id=0, has_side_effects=True, vmem_limit_bytes=32 * 2**20),
        cost_estimate=pl.CostEstimate(flops=10**10, bytes_accessed=2**25, transcendentals=0),
    )(high, low, orbitals)


def local(orbitals, occupations, rest_density, ionic_potential):
    points = orbitals.shape[3]
    pencil_rows = points // lax.axis_size("slab")
    basis = jnp.asarray(real_basis(points), jnp.float32)
    squared = jnp.asarray(wavenumbers_squared(points), jnp.float32)

    def product(spec, a, b):
        return jnp.einsum(spec, a, b, precision=lax.Precision.HIGHEST)

    kinetic_part = kinetic(orbitals)

    squares = orbitals[0] * orbitals[0] + orbitals[1] * orbitals[1]
    partial_sum = jnp.sum(occupations[:, None, None, None] * squares, axis=0)
    density = rest_density + lax.psum(partial_sum, "band")
    exchange_xc = -exchange_factor * jnp.cbrt(density)
    spectrum = product("xkz,jk->xjz", product("xyz,kz->xyk", density, basis), basis)
    spectrum = lax.all_to_all(spectrum, "slab", split_axis=1, concat_axis=0, tiled=True)
    own_squared = lax.dynamic_slice(squared, (lax.axis_index("slab") * pencil_rows,), (pencil_rows,))
    g2 = squared[:, None, None] + own_squared[None, :, None] + squared[None, None, :]
    positive = g2 > 0
    green = jnp.where(positive, 4.0 * math.pi / jnp.where(positive, g2, 1.0), 0.0)
    spectrum = product("xyz,kx->kyz", spectrum, basis) * green
    spectrum = product("kyz,kx->xyz", spectrum, basis)
    spectrum = lax.all_to_all(spectrum, "slab", split_axis=0, concat_axis=1, tiled=True)
    hartree = product("xkz,ky->xyz", product("xyk,kz->xyz", spectrum, basis), basis)
    potential = ionic_potential + hartree + exchange_xc

    applied = kinetic_part + potential * orbitals
    taylor_term = jnp.stack([time_step * applied[1], -time_step * applied[0]])
    return (taylor_term, potential)


def solution(mesh):
    return jax.shard_map(
        local,
        mesh=mesh,
        in_specs=(
            P(None, "band", "slab", None, None),
            P("band"),
            P("slab", None, None),
            P("slab", None, None),
        ),
        out_specs=(P(None, "band", "slab", None, None), P("slab", None, None)),
        check_vma=False,
    )
```

```python
import functools
import math

import jax
import jax.numpy as jnp
import numpy as np
from jax import lax
from jax.experimental import pallas as pl
from jax.experimental.pallas import tpu as pltpu
from jax.sharding import PartitionSpec as P

MESH = pl.DeviceIdType.MESH
grid_spacing = 0.4
time_step = 0.01
exchange_factor = (3.0 / math.pi) ** (1.0 / 3.0)
CHUNKS = 4


def wavenumbers_squared(points):
    indices = np.arange(points)
    signed = np.where(indices < points // 2, indices, indices - points)
    return (2.0 * math.pi / (points * grid_spacing) * signed) ** 2


def real_basis(points):
    j = np.arange(points)[:, None]
    x = np.arange(points)[None, :]
    cosine = np.cos(2.0 * math.pi * (j * x % points) / points)
    sine = np.sin(2.0 * math.pi * ((points - j) * x % points) / points)
    rows = np.where(j <= points // 2, cosine, sine) * math.sqrt(2.0 / points)
    return np.where((j == 0) | (j == points // 2), rows * math.sqrt(0.5), rows)


def kinetic_matrix(points):
    basis = real_basis(points)
    return basis.T @ (0.5 * wavenumbers_squared(points)[:, None] * basis)


def split(values):
    high = values.astype(jnp.bfloat16)
    return high, (values - high.astype(jnp.float32)).astype(jnp.bfloat16)


def dot(a, b):
    return jnp.dot(a, b, preferred_element_type=jnp.float32)


def left(matrix_high, matrix_low, values):
    high, low = split(values)
    return dot(jnp.concatenate([matrix_high, matrix_high], 1), jnp.concatenate([high, low], 0)) + dot(matrix_low, high)


def right(values, matrix_high, matrix_low):
    high, low = split(values)
    return dot(jnp.concatenate([high, low], 1), jnp.concatenate([matrix_high, matrix_high], 0)) + dot(high, matrix_low)


def exact(a, b):
    return jnp.dot(a, b, precision=lax.Precision.HIGHEST, preferred_element_type=jnp.float32)


def partner(me, step):
    step = lax.rem(step * 37, 64)
    y = lax.rem(me // 16 + step // 16, 4)
    x = lax.rem(lax.rem(me // 4, 4) + lax.rem(step // 4, 4), 4)
    return y * 16 + x * 4 + jnp.bitwise_xor(lax.rem(me, 4), lax.rem(step, 4))


def remote(source, target, send, recv, device):
    pltpu.make_async_remote_copy(
        src_ref=source, dst_ref=target, send_sem=send, recv_sem=recv, device_id=device, device_id_type=MESH
    ).start()


def wait_bytes(part, sem):
    pltpu.make_async_copy(part, part, sem).wait()


def kernel(
    high_ref, low_ref, basis_ref, basis_t_ref, occupations_ref, psi_hbm, rest_hbm, ionic_hbm, out_hbm, potential_ref,
    psi, pen, res, back, acc, rest, ionic, part, shares, density, spectrum, lines_in, lines_out, spectrum_back,
    load_sem, small_sem, out_sem, fwd_send, fwd_recv, bwd_send, bwd_recv, small_send, small_recv,
):
    band, me = lax.axis_index("band"), lax.axis_index("slab")
    points = psi.shape[-1]
    load = pltpu.make_async_copy(psi_hbm, psi, load_sem)
    load.start()
    load_rest = pltpu.make_async_copy(rest_hbm, rest, small_sem.at[0])
    load_rest.start()
    load_ionic = pltpu.make_async_copy(ionic_hbm, ionic, small_sem.at[1])
    load_ionic.start()
    barrier = pltpu.get_barrier_semaphore()

    @pl.loop(1, 64)
    def _(step):
        pl.semaphore_signal(barrier, inc=1, device_id=(band, partner(me, step)), device_id_type=MESH)

    for step in range(1, 4):
        pl.semaphore_signal(barrier, inc=1, device_id=(lax.rem(band + step, 4), me), device_id_type=MESH)

    load.wait()
    pl.semaphore_wait(barrier, 66)

    def field_part(ref, owner, c):
        rows = pl.ds(pl.multiple_of(owner // 4 * 8, 8), 8)
        return ref.at[:, lax.rem(owner, 4) * 4 + c, :, rows, :]

    def forward(c):
        @pl.loop(1, 64)
        def _(step):
            other = partner(me, step)
            remote(field_part(psi, other, c), pen.at[c, :, me], fwd_send.at[c], fwd_recv.at[c], (band, other))

        pltpu.make_async_copy(field_part(psi, me, c), pen.at[c, :, me], fwd_recv.at[c]).start()

    def backward(c):
        @pl.loop(1, 64)
        def _(step):
            other = partner(me, step)
            remote(res.at[c, :, other], field_part(back, me, c), bwd_send.at[c], bwd_recv.at[c], (band, other))

        pltpu.make_async_copy(res.at[c, :, me], field_part(back, me, c), bwd_recv.at[c]).start()

    def lines(c):
        wait_bytes(pen.at[c], fwd_recv.at[c])
        source, target = pen.reshape(CHUNKS, 2, 8 * points, points), res.reshape(CHUNKS, 2, 8 * points, points)
        for row in range(8):
            rows = pl.ds(row, points, stride=8)
            values = jnp.concatenate([source[c, 0, rows, :], source[c, 1, rows, :]], 1)
            values = left(high_ref[...], low_ref[...], values)
            target[c, 0, rows, :] = values[:, :points]
            target[c, 1, rows, :] = values[:, points:]

    def planes(c):
        @pl.loop(0, 8)
        def _(i):
            o, x = i // 2 * 4 + c, lax.rem(i, 2)
            real, imag = psi[0, o, x], psi[1, o, x]
            along_y = left(high_ref[...], low_ref[...], jnp.concatenate([real, imag], 1))
            along_z = right(jnp.concatenate([real, imag], 0), high_ref[...], low_ref[...])
            acc[0, o, x] = along_y[:, :points] + along_z[:points]
            acc[1, o, x] = along_y[:, points:] + along_z[points:]

    def finish(c):
        wait_bytes(pen.at[c], bwd_recv.at[c])

        @pl.loop(0, 8)
        def _(i):
            o, x = i // 2 * 4 + c, lax.rem(i, 2)
            potential = potential_ref[x]
            real = acc[0, o, x] + back[0, o, x] + potential * psi[0, o, x]
            imag = acc[1, o, x] + back[1, o, x] + potential * psi[1, o, x]
            acc[0, o, x] = imag
            acc[1, o, x] = -real
            pltpu.make_async_copy(acc.at[:, o, x], out_hbm.at[:, o, x], out_sem).start()

    def quarter(ref, owner):
        return ref.at[:, pl.ds(pl.multiple_of(owner * 32, 32), 32), :]

    def density_share():
        @pl.loop(0, 8)
        def _(i):
            x, rows = i // 4, pl.ds(pl.multiple_of(lax.rem(i, 4) * 32, 32), 32)
            total = jnp.zeros((32, points), jnp.float32)
            for o in range(16):
                real, imag = psi[0, o, x, rows, :], psi[1, o, x, rows, :]
                total = total + occupations_ref[o] * (real * real + imag * imag)
            part[x, rows, :] = total

        for step in range(1, 4):
            other = lax.rem(band + step, 4)
            remote(quarter(part, other), shares.at[step - 1], small_send.at[0], small_recv.at[0], (other, me))

    def density_sum():
        wait_bytes(shares, small_recv.at[0])
        load_rest.wait()
        rows = pl.ds(pl.multiple_of(band * 32, 32), 32)
        density[:, rows, :] = rest[:, rows, :] + (part[:, rows, :] + shares[0] + shares[1] + shares[2])
        for step in range(1, 4):
            other = lax.rem(band + step, 4)
            remote(quarter(density, band), quarter(density, band), small_send.at[1], small_recv.at[1], (other, me))

    def owner_of(block):
        return block * 4 + lax.rem(block, 4)

    block = me // 4
    owns = owner_of(block) == me

    def block_of(ref, i):
        return ref.at[:, pl.ds(pl.multiple_of(i * 8, 8), 8), :]

    def spectrum_send():
        wait_bytes(shares, small_recv.at[1])
        half = exact(density[...].reshape(2 * points, points), basis_t_ref[...])
        both = exact(basis_ref[...], jnp.concatenate([half[:points], half[points:]], 1))
        spectrum[0] = both[:, :points]
        spectrum[1] = both[:, points:]

        @pl.loop(0, 16)
        def _(i):
            i = lax.rem(i + block, 16)
            owner = owner_of(i)

            @pl.when(owner != me)
            def _():
                remote(block_of(spectrum, i), lines_in.at[me], small_send.at[2], small_recv.at[2], (band, owner))

            @pl.when(owner == me)
            def _():
                pltpu.make_async_copy(block_of(spectrum, i), lines_in.at[me], small_recv.at[2]).start()

    def hartree_lines():
        @pl.when(owns)
        def _():
            wait_bytes(lines_in, small_recv.at[2])
            source, target = lines_in.reshape(8 * points, points), lines_out.reshape(8 * points, points)

            def folded(i):
                return jnp.minimum(i, points - i)

            kx = folded(lax.broadcasted_iota(jnp.int32, (points, points), 0))
            kz = folded(lax.broadcasted_iota(jnp.int32, (points, points), 1))
            unit = 4.0 * math.pi * (points * grid_spacing / (2.0 * math.pi)) ** 2

            def green(row):
                ky = folded(block * 8 + row)
                square = kx * kx + kz * kz + ky * ky
                return jnp.where(square > 0, unit / jnp.maximum(square, 1).astype(jnp.float32), 0.0)

            for row in range(0, 8, 2):
                first, second = pl.ds(row, points, stride=8), pl.ds(row + 1, points, stride=8)
                values = exact(basis_ref[...], jnp.concatenate([source[first, :], source[second, :]], 1))
                values = values * jnp.concatenate([green(row), green(row + 1)], 1)
                values = exact(basis_t_ref[...], values)
                target[first, :] = values[:, :points]
                target[second, :] = values[:, points:]

            @pl.loop(1, 64)
            def _(step):
                other = partner(me, step)
                remote(lines_out.at[other], block_of(spectrum_back, block), small_send.at[3], small_recv.at[3], (band, other))

            pltpu.make_async_copy(lines_out.at[me], block_of(spectrum_back, block), small_recv.at[3]).start()

    def potential_sum():
        wait_bytes(spectrum_back, small_recv.at[3])
        half = exact(spectrum_back[...].reshape(2 * points, points), basis_ref[...])
        both = exact(basis_t_ref[...], jnp.concatenate([half[:points], half[points:]], 1))
        load_ionic.wait()
        for x in range(2):
            here = density[x]
            root = jnp.exp(jnp.log(here) * (1.0 / 3.0))
            root = root - (root * root * root - here) / (3.0 * root * root)
            potential_ref[x] = ionic[x] + both[:, x * points : (x + 1) * points] - exchange_factor * root

    forward(0)
    density_share()
    forward(1)
    planes(0)
    density_sum()
    forward(2)
    planes(1)
    spectrum_send()
    forward(3)
    lines(0)
    backward(0)
    hartree_lines()
    planes(2)
    lines(1)
    backward(1)
    planes(3)
    potential_sum()
    lines(2)
    backward(2)
    lines(3)
    backward(3)
    for c in range(CHUNKS):
        finish(c)

    for c in range(CHUNKS):
        wait_bytes(pen.at[c, :, pl.ds(0, 63)], fwd_send.at[c])
        wait_bytes(pen.at[c, :, pl.ds(0, 63)], bwd_send.at[c])
    wait_bytes(shares, small_send.at[0])
    wait_bytes(shares, small_send.at[1])

    @pl.when(owns)
    def _():
        wait_bytes(lines_in.at[pl.ds(0, 15)], small_send.at[2])
        wait_bytes(lines_in.at[pl.ds(0, 63)], small_send.at[3])

    @pl.when(jnp.logical_not(owns))
    def _():
        wait_bytes(lines_in.at[pl.ds(0, 16)], small_send.at[2])

    pltpu.make_async_copy(acc, out_hbm, out_sem).wait()


def local(orbitals, occupations, rest_density, ionic_potential):
    points = orbitals.shape[3]
    high, low = split(jnp.asarray(kinetic_matrix(points), jnp.float32))
    basis = real_basis(points)
    slab_shape = rest_density.shape
    field, slab = pltpu.VMEM(orbitals.shape, jnp.float32), pltpu.VMEM(slab_shape, jnp.float32)
    pencil = pltpu.VMEM((CHUNKS, 2, 64, 2, 8, points), jnp.float32)
    lines = pltpu.VMEM((64, 2, 8, points), jnp.float32)
    dma = pltpu.SemaphoreType.DMA
    in_vmem, anywhere = pl.BlockSpec(memory_space=pltpu.VMEM), pl.BlockSpec(memory_space=pl.ANY)
    applied, potential = pl.pallas_call(
        kernel,
        out_shape=(
            jax.ShapeDtypeStruct(orbitals.shape, jnp.float32),
            jax.ShapeDtypeStruct(slab_shape, jnp.float32),
        ),
        in_specs=[in_vmem] * 4 + [pl.BlockSpec(memory_space=pltpu.SMEM)] + [anywhere] * 3,
        out_specs=(anywhere, in_vmem),
        scratch_shapes=[
            field, pencil, pencil, field, field, slab, slab, slab,
            pltpu.VMEM((3, 2, 32, points), jnp.float32), slab, slab, lines, lines, slab,
            dma, dma((2,)), dma, dma((CHUNKS,)), dma((CHUNKS,)), dma((CHUNKS,)), dma((CHUNKS,)), dma((4,)), dma((4,)),
        ],
        compiler_params=pltpu.CompilerParams(collective_id=0, has_side_effects=True, vmem_limit_bytes=40 * 2**20),
        cost_estimate=pl.CostEstimate(flops=10**10, bytes_accessed=2**25, transcendentals=0),
    )(
        high, low, jnp.asarray(basis, jnp.float32), jnp.asarray(basis.T, jnp.float32),
        occupations, orbitals, rest_density, ionic_potential,
    )
    return (time_step * applied, potential)


def solution(mesh):
    return jax.shard_map(
        local,
        mesh=mesh,
        in_specs=(
            P(None, "band", "slab", None, None),
            P("band"),
            P("slab", None, None),
            P("slab", None, None),
        ),
        out_specs=(P(None, "band", "slab", None, None), P("slab", None, None)),
        check_vma=False,
    )
```

```python
import functools
import math

import jax
import jax.numpy as jnp
import numpy as np
from jax import lax
from jax.experimental import pallas as pl
from jax.experimental.pallas import tpu as pltpu
from jax.sharding import PartitionSpec as P

MESH = pl.DeviceIdType.MESH
grid_spacing = 0.4
time_step = 0.01
exchange_factor = (3.0 / math.pi) ** (1.0 / 3.0)
CHUNKS = 4


def wavenumbers_squared(points):
    indices = np.arange(points)
    signed = np.where(indices < points // 2, indices, indices - points)
    return (2.0 * math.pi / (points * grid_spacing) * signed) ** 2


def real_basis(points):
    j = np.arange(points)[:, None]
    x = np.arange(points)[None, :]
    cosine = np.cos(2.0 * math.pi * (j * x % points) / points)
    sine = np.sin(2.0 * math.pi * ((points - j) * x % points) / points)
    rows = np.where(j <= points // 2, cosine, sine) * math.sqrt(2.0 / points)
    return np.where((j == 0) | (j == points // 2), rows * math.sqrt(0.5), rows)


def kinetic_matrix(points):
    basis = real_basis(points)
    return basis.T @ (0.5 * wavenumbers_squared(points)[:, None] * basis)


def split(values):
    high = values.astype(jnp.bfloat16)
    return high, (values - high.astype(jnp.float32)).astype(jnp.bfloat16)


def dot(a, b):
    return jnp.dot(a, b, preferred_element_type=jnp.float32)


def left(matrix_high, matrix_low, values):
    high, low = split(values)
    return dot(jnp.concatenate([matrix_high, matrix_high], 1), jnp.concatenate([high, low], 0)) + dot(matrix_low, high)


def right(values, matrix_high, matrix_low):
    high, low = split(values)
    return dot(jnp.concatenate([high, low], 1), jnp.concatenate([matrix_high, matrix_high], 0)) + dot(high, matrix_low)


def exact(a, b):
    return jnp.dot(a, b, precision=lax.Precision.HIGHEST, preferred_element_type=jnp.float32)


def partner(me, step):
    step = lax.rem(step * 37, 64)
    y = lax.rem(me // 16 + step // 16, 4)
    x = lax.rem(lax.rem(me // 4, 4) + lax.rem(step // 4, 4), 4)
    return y * 16 + x * 4 + jnp.bitwise_xor(lax.rem(me, 4), lax.rem(step, 4))


def remote(source, target, send, recv, device):
    pltpu.make_async_remote_copy(
        src_ref=source, dst_ref=target, send_sem=send, recv_sem=recv, device_id=device, device_id_type=MESH
    ).start()


def wait_bytes(part, sem):
    pltpu.make_async_copy(part, part, sem).wait()


def kernel(
    tables_hbm, occupations_ref, psi_hbm, rest_hbm, ionic_hbm, acc, potential_ref,
    tables, high_ref, low_ref, psi, pen, res, back, rest, ionic, part, shares, density, spectrum, lines_in, lines_out, spectrum_back,
    load_sem, small_sem, fwd_send, fwd_recv, bwd_send, bwd_recv, small_send, small_recv,
):
    band, me = lax.axis_index("band"), lax.axis_index("slab")
    points = psi.shape[-1]
    barrier = pltpu.get_barrier_semaphore()

    @pl.loop(1, 64)
    def _(step):
        pl.semaphore_signal(barrier, inc=1, device_id=(band, partner(me, step)), device_id_type=MESH)

    for step in range(1, 4):
        pl.semaphore_signal(barrier, inc=1, device_id=(lax.rem(band + step, 4), me), device_id_type=MESH)

    basis_ref, basis_t_ref = tables.at[0], tables.at[1]
    def load(c):
        for group in range(4):
            o = group * 4 + c
            pltpu.make_async_copy(psi_hbm.at[:, o], psi.at[:, o], load_sem.at[c]).start()

    for c in range(CHUNKS):
        load(c)
    load_rest = pltpu.make_async_copy(rest_hbm, rest, small_sem.at[0])
    load_rest.start()
    load_tables = pltpu.make_async_copy(tables_hbm, tables, small_sem.at[2])
    load_tables.start()
    load_ionic = pltpu.make_async_copy(ionic_hbm, ionic, small_sem.at[1])
    load_ionic.start()
    wait_bytes(pen.at[0], load_sem.at[0])
    pl.semaphore_wait(barrier, 66)

    def field_part(ref, owner, c):
        rows = pl.ds(pl.multiple_of(owner // 4 * 8, 8), 8)
        return ref.at[:, lax.rem(owner, 4) * 4 + c, :, rows, :]

    def forward(c):
        @pl.loop(1, 64)
        def _(step):
            other = partner(me, step)
            remote(field_part(psi, other, c), pen.at[c, :, me], fwd_send.at[c], fwd_recv.at[c], (band, other))

        pltpu.make_async_copy(field_part(psi, me, c), pen.at[c, :, me], fwd_recv.at[c]).start()

    def backward(c):
        @pl.loop(1, 64)
        def _(step):
            other = partner(me, step)
            remote(res.at[c, :, other], field_part(back, me, c), bwd_send.at[c], bwd_recv.at[c], (band, other))

        pltpu.make_async_copy(res.at[c, :, me], field_part(back, me, c), bwd_recv.at[c]).start()

    def lines(c):
        wait_bytes(pen.at[c], fwd_recv.at[c])
        source, target = pen.reshape(CHUNKS, 2, 8 * points, points), res.reshape(CHUNKS, 2, 8 * points, points)
        for row in range(8):
            rows = pl.ds(row, points, stride=8)
            values = jnp.concatenate([source[c, 0, rows, :], source[c, 1, rows, :]], 1)
            values = left(high_ref[...], low_ref[...], values)
            target[c, 0, rows, :] = values[:, :points]
            target[c, 1, rows, :] = values[:, points:]

    def planes(c):
        @pl.loop(0, 8)
        def _(i):
            o, x = i // 2 * 4 + c, lax.rem(i, 2)
            real, imag = psi[0, o, x], psi[1, o, x]
            along_y = left(high_ref[...], low_ref[...], jnp.concatenate([real, imag], 1))
            along_z = right(jnp.concatenate([real, imag], 0), high_ref[...], low_ref[...])
            acc[0, o, x] = along_y[:, :points] + along_z[:points]
            acc[1, o, x] = along_y[:, points:] + along_z[points:]

    def finish(c):
        wait_bytes(pen.at[c], bwd_recv.at[c])

        @pl.loop(0, 8)
        def _(i):
            o, x = i // 2 * 4 + c, lax.rem(i, 2)
            potential = potential_ref[x]
            real = acc[0, o, x] + back[0, o, x] + potential * psi[0, o, x]
            imag = acc[1, o, x] + back[1, o, x] + potential * psi[1, o, x]
            acc[0, o, x] = time_step * imag
            acc[1, o, x] = -time_step * real

    def quarter(ref, owner):
        return ref.at[:, pl.ds(pl.multiple_of(owner * 32, 32), 32), :]

    def density_share():
        @pl.loop(0, 8)
        def _(i):
            x, rows = i // 4, pl.ds(pl.multiple_of(lax.rem(i, 4) * 32, 32), 32)
            total = jnp.zeros((32, points), jnp.float32)
            for o in range(16):
                real, imag = psi[0, o, x, rows, :], psi[1, o, x, rows, :]
                total = total + occupations_ref[o] * (real * real + imag * imag)
            part[x, rows, :] = total

        for step in range(1, 4):
            other = lax.rem(band + step, 4)
            remote(quarter(part, other), shares.at[step - 1], small_send.at[0], small_recv.at[0], (other, me))

    def density_sum():
        wait_bytes(shares, small_recv.at[0])
        load_rest.wait()
        rows = pl.ds(pl.multiple_of(band * 32, 32), 32)
        density[:, rows, :] = rest[:, rows, :] + (part[:, rows, :] + shares[0] + shares[1] + shares[2])
        for step in range(1, 4):
            other = lax.rem(band + step, 4)
            remote(quarter(density, band), quarter(density, band), small_send.at[1], small_recv.at[1], (other, me))

    def owner_of(block):
        return block * 4 + lax.rem(block, 4)

    block = me // 4
    owns = owner_of(block) == me

    def block_of(ref, i):
        return ref.at[:, pl.ds(pl.multiple_of(i * 8, 8), 8), :]

    def spectrum_send():
        wait_bytes(shares, small_recv.at[1])
        half = exact(density[...].reshape(2 * points, points), basis_t_ref[...])
        both = exact(basis_ref[...], jnp.concatenate([half[:points], half[points:]], 1))
        spectrum[0] = both[:, :points]
        spectrum[1] = both[:, points:]

        @pl.loop(0, 16)
        def _(i):
            i = lax.rem(i + block, 16)
            owner = owner_of(i)

            @pl.when(owner != me)
            def _():
                remote(block_of(spectrum, i), lines_in.at[me], small_send.at[2], small_recv.at[2], (band, owner))

            @pl.when(owner == me)
            def _():
                pltpu.make_async_copy(block_of(spectrum, i), lines_in.at[me], small_recv.at[2]).start()

    def hartree_lines():
        @pl.when(owns)
        def _():
            wait_bytes(lines_in, small_recv.at[2])
            source, target = lines_in.reshape(8 * points, points), lines_out.reshape(8 * points, points)

            def folded(i):
                return jnp.minimum(i, points - i)

            kx = folded(lax.broadcasted_iota(jnp.int32, (points, points), 0))
            kz = folded(lax.broadcasted_iota(jnp.int32, (points, points), 1))
            unit = 4.0 * math.pi * (points * grid_spacing / (2.0 * math.pi)) ** 2

            def green(row):
                ky = folded(block * 8 + row)
                square = kx * kx + kz * kz + ky * ky
                return jnp.where(square > 0, unit / jnp.maximum(square, 1).astype(jnp.float32), 0.0)

            for row in range(0, 8, 2):
                first, second = pl.ds(row, points, stride=8), pl.ds(row + 1, points, stride=8)
                values = exact(basis_ref[...], jnp.concatenate([source[first, :], source[second, :]], 1))
                values = values * jnp.concatenate([green(row), green(row + 1)], 1)
                values = exact(basis_t_ref[...], values)
                target[first, :] = values[:, :points]
                target[second, :] = values[:, points:]

            @pl.loop(1, 64)
            def _(step):
                other = partner(me, step)
                remote(lines_out.at[other], block_of(spectrum_back, block), small_send.at[3], small_recv.at[3], (band, other))

            pltpu.make_async_copy(lines_out.at[me], block_of(spectrum_back, block), small_recv.at[3]).start()

    def potential_sum():
        wait_bytes(spectrum_back, small_recv.at[3])
        half = exact(spectrum_back[...].reshape(2 * points, points), basis_ref[...])
        both = exact(basis_t_ref[...], jnp.concatenate([half[:points], half[points:]], 1))
        load_ionic.wait()
        for x in range(2):
            here = density[x]
            root = jnp.exp(jnp.log(here) * (1.0 / 3.0))
            root = root - (root * root * root - here) / (3.0 * root * root)
            potential_ref[x] = ionic[x] + both[:, x * points : (x + 1) * points] - exchange_factor * root

    forward(0)
    for c in range(1, CHUNKS):
        wait_bytes(pen.at[0], load_sem.at[c])
    load_tables.wait()
    high_ref[...], low_ref[...] = split(tables[2])
    density_share()
    forward(1)
    planes(0)
    density_sum()
    forward(2)
    planes(1)
    spectrum_send()
    forward(3)
    lines(0)
    backward(0)
    hartree_lines()
    planes(2)
    lines(1)
    backward(1)
    planes(3)
    potential_sum()
    lines(2)
    backward(2)
    lines(3)
    backward(3)
    for c in range(CHUNKS):
        finish(c)

    for c in range(CHUNKS):
        wait_bytes(pen.at[c, :, pl.ds(0, 63)], fwd_send.at[c])
        wait_bytes(pen.at[c, :, pl.ds(0, 63)], bwd_send.at[c])
    wait_bytes(shares, small_send.at[0])
    wait_bytes(shares, small_send.at[1])

    @pl.when(owns)
    def _():
        wait_bytes(lines_in.at[pl.ds(0, 15)], small_send.at[2])
        wait_bytes(lines_in.at[pl.ds(0, 63)], small_send.at[3])

    @pl.when(jnp.logical_not(owns))
    def _():
        wait_bytes(lines_in.at[pl.ds(0, 16)], small_send.at[2])


def pass_on(applied, potential, out_hbm, potential_out_hbm, sems):
    copies = [
        pltpu.make_async_copy(applied.at[p, pl.ds(o, 4)], out_hbm.at[p, pl.ds(o, 4)], sems.at[p * 4 + o // 4])
        for p in range(2)
        for o in range(0, 16, 4)
    ]
    copies.append(pltpu.make_async_copy(potential, potential_out_hbm, sems.at[8]))
    for copy in copies:
        copy.start()
    for copy in copies:
        copy.wait()


def local(orbitals, occupations, rest_density, ionic_potential):
    points = orbitals.shape[3]
    basis = real_basis(points)
    tables = np.stack([basis, basis.T, kinetic_matrix(points)])
    slab_shape = rest_density.shape
    field, slab = pltpu.VMEM(orbitals.shape, jnp.float32), pltpu.VMEM(slab_shape, jnp.float32)
    pencil = pltpu.VMEM((CHUNKS, 2, 64, 2, 8, points), jnp.float32)
    lines = pltpu.VMEM((64, 2, 8, points), jnp.float32)
    dma = pltpu.SemaphoreType.DMA
    in_vmem, anywhere = pl.BlockSpec(memory_space=pltpu.VMEM), pl.BlockSpec(memory_space=pl.ANY)
    applied, potential = pl.pallas_call(
        kernel,
        out_shape=(
            pltpu.VMEM(orbitals.shape, jnp.float32),
            pltpu.VMEM(slab_shape, jnp.float32),
        ),
        in_specs=[anywhere, pl.BlockSpec(memory_space=pltpu.SMEM), anywhere, anywhere, anywhere],
        out_specs=(in_vmem, in_vmem),
        scratch_shapes=[
            pltpu.VMEM(tables.shape, jnp.float32),
            pltpu.VMEM((points, points), jnp.bfloat16), pltpu.VMEM((points, points), jnp.bfloat16), field, pencil, pencil, field, slab, slab, slab,
            pltpu.VMEM((3, 2, 32, points), jnp.float32), slab, slab, lines, lines, slab,
            dma((CHUNKS,)), dma((3,)), dma((CHUNKS,)), dma((CHUNKS,)), dma((CHUNKS,)), dma((CHUNKS,)), dma((4,)), dma((4,)),
        ],
        compiler_params=pltpu.CompilerParams(collective_id=0, has_side_effects=True, vmem_limit_bytes=58 * 2**20),
        cost_estimate=pl.CostEstimate(flops=10**10, bytes_accessed=2**25, transcendentals=0),
    )(
        jnp.asarray(tables, jnp.float32), occupations, orbitals, rest_density, ionic_potential,
    )
    return pl.pallas_call(
        pass_on,
        out_shape=(
            jax.ShapeDtypeStruct(orbitals.shape, jnp.float32),
            jax.ShapeDtypeStruct(slab_shape, jnp.float32),
        ),
        in_specs=[anywhere] * 2,
        out_specs=(anywhere, anywhere),
        scratch_shapes=[dma((9,))],
        compiler_params=pltpu.CompilerParams(vmem_limit_bytes=2**20),
    )(applied, potential)


def solution(mesh):
    return jax.shard_map(
        local,
        mesh=mesh,
        in_specs=(
            P(None, "band", "slab", None, None),
            P("band"),
            P("slab", None, None),
            P("slab", None, None),
        ),
        out_specs=(P(None, "band", "slab", None, None), P("slab", None, None)),
        check_vma=False,
    )
```

```python
import functools
import math

import jax
import jax.numpy as jnp
import numpy as np
from jax import lax
from jax.experimental import pallas as pl
from jax.experimental.pallas import tpu as pltpu
from jax.sharding import PartitionSpec as P

MESH = pl.DeviceIdType.MESH
grid_spacing = 0.4
time_step = 0.01
exchange_factor = (3.0 / math.pi) ** (1.0 / 3.0)
CHUNKS = 4


def wavenumbers_squared(points):
    indices = np.arange(points)
    signed = np.where(indices < points // 2, indices, indices - points)
    return (2.0 * math.pi / (points * grid_spacing) * signed) ** 2


def real_basis(points):
    j = np.arange(points)[:, None]
    x = np.arange(points)[None, :]
    cosine = np.cos(2.0 * math.pi * (j * x % points) / points)
    sine = np.sin(2.0 * math.pi * ((points - j) * x % points) / points)
    rows = np.where(j <= points // 2, cosine, sine) * math.sqrt(2.0 / points)
    return np.where((j == 0) | (j == points // 2), rows * math.sqrt(0.5), rows)


def kinetic_matrix(points):
    basis = real_basis(points)
    return basis.T @ (0.5 * wavenumbers_squared(points)[:, None] * basis)


def split(values):
    high = values.astype(jnp.bfloat16)
    return high, (values - high.astype(jnp.float32)).astype(jnp.bfloat16)


def dot(a, b):
    return jnp.dot(a, b, preferred_element_type=jnp.float32)


def left(matrix_high, matrix_low, values):
    high, low = split(values)
    return dot(jnp.concatenate([matrix_high, matrix_high], 1), jnp.concatenate([high, low], 0)) + dot(matrix_low, high)


def right(values, matrix_high, matrix_low):
    high, low = split(values)
    return dot(jnp.concatenate([high, low], 1), jnp.concatenate([matrix_high, matrix_high], 0)) + dot(high, matrix_low)


def exact(a, b):
    return jnp.dot(a, b, precision=lax.Precision.HIGHEST, preferred_element_type=jnp.float32)


def partner(me, step):
    step = lax.rem(step * 37, 64)
    y = lax.rem(me // 16 + step // 16, 4)
    x = lax.rem(lax.rem(me // 4, 4) + lax.rem(step // 4, 4), 4)
    return y * 16 + x * 4 + jnp.bitwise_xor(lax.rem(me, 4), lax.rem(step, 4))


def remote(source, target, send, recv, device):
    pltpu.make_async_remote_copy(
        src_ref=source, dst_ref=target, send_sem=send, recv_sem=recv, device_id=device, device_id_type=MESH
    ).start()


def wait_bytes(part, sem):
    pltpu.make_async_copy(part, part, sem).wait()


def kernel(
    tables_hbm, occupations_ref, psi_hbm, rest_hbm, ionic_hbm, acc, potential_ref,
    tables, high_ref, low_ref, psi, pen, res, back, rest, ionic, part, relay, shares, density, spectrum, lines_in, lines_out, spectrum_back,
    load_sem, small_sem, fwd_send, fwd_recv, bwd_send, bwd_recv, small_send, small_recv,
):
    band, me = lax.axis_index("band"), lax.axis_index("slab")
    points = psi.shape[-1]
    barrier = pltpu.get_barrier_semaphore()

    @pl.loop(1, 64)
    def _(step):
        pl.semaphore_signal(barrier, inc=1, device_id=(band, partner(me, step)), device_id_type=MESH)

    for step in range(1, 4):
        pl.semaphore_signal(barrier, inc=1, device_id=(lax.rem(band + step, 4), me), device_id_type=MESH)

    basis_ref, basis_t_ref = tables.at[0], tables.at[1]
    def load(c):
        for group in range(4):
            o = group * 4 + c
            pltpu.make_async_copy(psi_hbm.at[:, o], psi.at[:, o], load_sem.at[c]).start()

    for c in range(CHUNKS):
        load(c)
    load_rest = pltpu.make_async_copy(rest_hbm, rest, small_sem.at[0])
    load_rest.start()
    load_tables = pltpu.make_async_copy(tables_hbm, tables, small_sem.at[2])
    load_tables.start()
    load_ionic = pltpu.make_async_copy(ionic_hbm, ionic, small_sem.at[1])
    load_ionic.start()
    wait_bytes(pen.at[0], load_sem.at[0])
    pl.semaphore_wait(barrier, 66)

    def field_part(ref, owner, c):
        rows = pl.ds(pl.multiple_of(owner // 4 * 8, 8), 8)
        return ref.at[:, lax.rem(owner, 4) * 4 + c, :, rows, :]

    def forward(c):
        @pl.loop(1, 64)
        def _(step):
            other = partner(me, step)
            remote(field_part(psi, other, c), pen.at[c, :, me], fwd_send.at[c], fwd_recv.at[c], (band, other))

        pltpu.make_async_copy(field_part(psi, me, c), pen.at[c, :, me], fwd_recv.at[c]).start()

    def backward(c):
        @pl.loop(1, 64)
        def _(step):
            other = partner(me, step)
            remote(res.at[c, :, other], field_part(back, me, c), bwd_send.at[c], bwd_recv.at[c], (band, other))

        pltpu.make_async_copy(res.at[c, :, me], field_part(back, me, c), bwd_recv.at[c]).start()

    def lines(c):
        wait_bytes(pen.at[c], fwd_recv.at[c])
        source, target = pen.reshape(CHUNKS, 2, 8 * points, points), res.reshape(CHUNKS, 2, 8 * points, points)
        for row in range(8):
            rows = pl.ds(row, points, stride=8)
            values = jnp.concatenate([source[c, 0, rows, :], source[c, 1, rows, :]], 1)
            values = left(high_ref[...], low_ref[...], values)
            target[c, 0, rows, :] = values[:, :points]
            target[c, 1, rows, :] = values[:, points:]

    def planes(c):
        @pl.loop(0, 8)
        def _(i):
            o, x = i // 2 * 4 + c, lax.rem(i, 2)
            real, imag = psi[0, o, x], psi[1, o, x]
            along_y = left(high_ref[...], low_ref[...], jnp.concatenate([real, imag], 1))
            along_z = right(jnp.concatenate([real, imag], 0), high_ref[...], low_ref[...])
            acc[0, o, x] = along_y[:, :points] + along_z[:points]
            acc[1, o, x] = along_y[:, points:] + along_z[points:]

    def finish(c):
        wait_bytes(pen.at[c], bwd_recv.at[c])

        @pl.loop(0, 8)
        def _(i):
            o, x = i // 2 * 4 + c, lax.rem(i, 2)
            potential = potential_ref[x]
            real = acc[0, o, x] + back[0, o, x] + potential * psi[0, o, x]
            imag = acc[1, o, x] + back[1, o, x] + potential * psi[1, o, x]
            acc[0, o, x] = time_step * imag
            acc[1, o, x] = -time_step * real

    after, before, across = lax.rem(band + 1, 4), lax.rem(band + 3, 4), lax.rem(band + 2, 4)

    def rows_of(owner, start, size):
        return pl.ds(pl.multiple_of(owner * 32 + start, 16), size)

    def rows_in(ref, owner, start, size):
        return ref.at[:, rows_of(owner, start, size), :]

    def density_share():
        @pl.loop(0, 8)
        def _(i):
            x, rows = i // 4, pl.ds(pl.multiple_of(lax.rem(i, 4) * 32, 32), 32)
            total = jnp.zeros((32, points), jnp.float32)
            for o in range(16):
                real, imag = psi[0, o, x, rows, :], psi[1, o, x, rows, :]
                total = total + occupations_ref[o] * (real * real + imag * imag)
            part[x, rows, :] = total

        remote(rows_in(part, across, 0, 16), relay.at[0], small_send.at[0], small_recv.at[0], (after, me))
        remote(rows_in(part, across, 16, 16), relay.at[1], small_send.at[0], small_recv.at[0], (before, me))

    def density_relay():
        wait_bytes(relay, small_recv.at[0])
        first, second = rows_of(after, 0, 16), rows_of(before, 16, 16)
        part[:, first, :] = part[:, first, :] + relay[0]
        part[:, second, :] = part[:, second, :] + relay[1]
        remote(rows_in(part, after, 0, 32), shares.at[0], small_send.at[1], small_recv.at[1], (after, me))
        remote(rows_in(part, before, 0, 32), shares.at[1], small_send.at[1], small_recv.at[1], (before, me))

    def density_sum():
        wait_bytes(shares, small_recv.at[1])
        load_rest.wait()
        rows = rows_of(band, 0, 32)
        density[:, rows, :] = rest[:, rows, :] + (part[:, rows, :] + shares[0] + shares[1])
        own = rows_in(density, band, 0, 32)
        remote(own, own, small_send.at[2], small_recv.at[2], (after, me))
        remote(own, own, small_send.at[2], small_recv.at[2], (before, me))

    def density_spread():
        wait_bytes(shares, small_recv.at[2])
        first, second = rows_in(density, before, 0, 16), rows_in(density, after, 16, 16)
        remote(first, first, small_send.at[3], small_recv.at[3], (after, me))
        remote(second, second, small_send.at[3], small_recv.at[3], (before, me))

    def owner_of(block):
        return block * 4 + lax.rem(block, 4)

    block = me // 4
    owns = owner_of(block) == me

    def block_of(ref, i):
        return ref.at[:, pl.ds(pl.multiple_of(i * 8, 8), 8), :]

    def spectrum_send():
        wait_bytes(relay, small_recv.at[3])
        half = exact(density[...].reshape(2 * points, points), basis_t_ref[...])
        both = exact(basis_ref[...], jnp.concatenate([half[:points], half[points:]], 1))
        spectrum[0] = both[:, :points]
        spectrum[1] = both[:, points:]

        @pl.loop(0, 16)
        def _(i):
            i = lax.rem(i + block, 16)
            owner = owner_of(i)

            @pl.when(owner != me)
            def _():
                remote(block_of(spectrum, i), lines_in.at[me], small_send.at[4], small_recv.at[4], (band, owner))

            @pl.when(owner == me)
            def _():
                pltpu.make_async_copy(block_of(spectrum, i), lines_in.at[me], small_recv.at[4]).start()

    def hartree_lines():
        @pl.when(owns)
        def _():
            wait_bytes(lines_in, small_recv.at[4])
            source, target = lines_in.reshape(8 * points, points), lines_out.reshape(8 * points, points)

            def folded(i):
                return jnp.minimum(i, points - i)

            kx = folded(lax.broadcasted_iota(jnp.int32, (points, points), 0))
            kz = folded(lax.broadcasted_iota(jnp.int32, (points, points), 1))
            unit = 4.0 * math.pi * (points * grid_spacing / (2.0 * math.pi)) ** 2

            def green(row):
                ky = folded(block * 8 + row)
                square = kx * kx + kz * kz + ky * ky
                return jnp.where(square > 0, unit / jnp.maximum(square, 1).astype(jnp.float32), 0.0)

            for row in range(0, 8, 2):
                first, second = pl.ds(row, points, stride=8), pl.ds(row + 1, points, stride=8)
                values = exact(basis_ref[...], jnp.concatenate([source[first, :], source[second, :]], 1))
                values = values * jnp.concatenate([green(row), green(row + 1)], 1)
                values = exact(basis_t_ref[...], values)
                target[first, :] = values[:, :points]
                target[second, :] = values[:, points:]

            @pl.loop(1, 64)
            def _(step):
                other = partner(me, step)
                remote(lines_out.at[other], block_of(spectrum_back, block), small_send.at[5], small_recv.at[5], (band, other))

            pltpu.make_async_copy(lines_out.at[me], block_of(spectrum_back, block), small_recv.at[5]).start()

    def potential_sum():
        wait_bytes(spectrum_back, small_recv.at[5])
        half = exact(spectrum_back[...].reshape(2 * points, points), basis_ref[...])
        both = exact(basis_t_ref[...], jnp.concatenate([half[:points], half[points:]], 1))
        load_ionic.wait()
        for x in range(2):
            here = density[x]
            root = jnp.exp(jnp.log(here) * (1.0 / 3.0))
            root = root - (root * root * root - here) / (3.0 * root * root)
            potential_ref[x] = ionic[x] + both[:, x * points : (x + 1) * points] - exchange_factor * root

    forward(0)
    for c in range(1, CHUNKS):
        wait_bytes(pen.at[0], load_sem.at[c])
    load_tables.wait()
    high_ref[...], low_ref[...] = split(tables[2])
    density_share()
    forward(1)
    planes(0)
    density_relay()
    forward(2)
    planes(1)
    density_sum()
    forward(3)
    planes(2)
    density_spread()
    lines(0)
    backward(0)
    planes(3)
    spectrum_send()
    lines(1)
    backward(1)
    hartree_lines()
    lines(2)
    backward(2)
    lines(3)
    backward(3)
    potential_sum()
    finish(0)
    finish(1)
    finish(2)
    finish(3)
    for c in range(CHUNKS):
        wait_bytes(pen.at[c, :, pl.ds(0, 63)], fwd_send.at[c])
        wait_bytes(pen.at[c, :, pl.ds(0, 63)], bwd_send.at[c])
    wait_bytes(relay, small_send.at[0])
    wait_bytes(shares, small_send.at[1])
    wait_bytes(shares, small_send.at[2])
    wait_bytes(relay, small_send.at[3])

    @pl.when(owns)
    def _():
        wait_bytes(lines_in.at[pl.ds(0, 15)], small_send.at[4])
        wait_bytes(lines_in.at[pl.ds(0, 63)], small_send.at[5])

    @pl.when(jnp.logical_not(owns))
    def _():
        wait_bytes(lines_in.at[pl.ds(0, 16)], small_send.at[4])


def pass_on(applied, potential, out_hbm, potential_out_hbm, sems):
    copies = [
        pltpu.make_async_copy(applied.at[p, pl.ds(o, 4)], out_hbm.at[p, pl.ds(o, 4)], sems.at[p * 4 + o // 4])
        for p in range(2)
        for o in range(0, 16, 4)
    ]
    copies.append(pltpu.make_async_copy(potential, potential_out_hbm, sems.at[8]))
    for copy in copies:
        copy.start()
    for copy in copies:
        copy.wait()


def local(orbitals, occupations, rest_density, ionic_potential):
    points = orbitals.shape[3]
    basis = real_basis(points)
    tables = np.stack([basis, basis.T, kinetic_matrix(points)])
    slab_shape = rest_density.shape
    field, slab = pltpu.VMEM(orbitals.shape, jnp.float32), pltpu.VMEM(slab_shape, jnp.float32)
    pencil = pltpu.VMEM((CHUNKS, 2, 64, 2, 8, points), jnp.float32)
    lines = pltpu.VMEM((64, 2, 8, points), jnp.float32)
    dma = pltpu.SemaphoreType.DMA
    in_vmem, anywhere = pl.BlockSpec(memory_space=pltpu.VMEM), pl.BlockSpec(memory_space=pl.ANY)
    applied, potential = pl.pallas_call(
        kernel,
        out_shape=(
            pltpu.VMEM(orbitals.shape, jnp.float32),
            pltpu.VMEM(slab_shape, jnp.float32),
        ),
        in_specs=[anywhere, pl.BlockSpec(memory_space=pltpu.SMEM), anywhere, anywhere, anywhere],
        out_specs=(in_vmem, in_vmem),
        scratch_shapes=[
            pltpu.VMEM(tables.shape, jnp.float32),
            pltpu.VMEM((points, points), jnp.bfloat16), pltpu.VMEM((points, points), jnp.bfloat16), field, pencil, pencil, field, slab, slab, slab,
            pltpu.VMEM((2, 2, 16, points), jnp.float32), pltpu.VMEM((2, 2, 32, points), jnp.float32), slab, slab, lines, lines, slab,
            dma((CHUNKS,)), dma((3,)), dma((CHUNKS,)), dma((CHUNKS,)), dma((CHUNKS,)), dma((CHUNKS,)), dma((6,)), dma((6,)),
        ],
        compiler_params=pltpu.CompilerParams(collective_id=0, has_side_effects=True, vmem_limit_bytes=58 * 2**20),
        cost_estimate=pl.CostEstimate(flops=10**10, bytes_accessed=2**25, transcendentals=0),
    )(
        jnp.asarray(tables, jnp.float32), occupations, orbitals, rest_density, ionic_potential,
    )
    return pl.pallas_call(
        pass_on,
        out_shape=(
            jax.ShapeDtypeStruct(orbitals.shape, jnp.float32),
            jax.ShapeDtypeStruct(slab_shape, jnp.float32),
        ),
        in_specs=[anywhere] * 2,
        out_specs=(anywhere, anywhere),
        scratch_shapes=[dma((9,))],
        compiler_params=pltpu.CompilerParams(vmem_limit_bytes=2**20),
    )(applied, potential)


def solution(mesh):
    return jax.shard_map(
        local,
        mesh=mesh,
        in_specs=(
            P(None, "band", "slab", None, None),
            P("band"),
            P("slab", None, None),
            P("slab", None, None),
        ),
        out_specs=(P(None, "band", "slab", None, None), P("slab", None, None)),
        check_vma=False,
    )
```

```python
import functools
import math

import jax
import jax.numpy as jnp
import numpy as np
from jax import lax
from jax.experimental import pallas as pl
from jax.experimental.pallas import tpu as pltpu
from jax.sharding import PartitionSpec as P

MESH = pl.DeviceIdType.MESH
grid_spacing = 0.4
time_step = 0.01
exchange_factor = (3.0 / math.pi) ** (1.0 / 3.0)
CHUNKS = 4


def wavenumbers_squared(points):
    indices = np.arange(points)
    signed = np.where(indices < points // 2, indices, indices - points)
    return (2.0 * math.pi / (points * grid_spacing) * signed) ** 2


def real_basis(points):
    j = np.arange(points)[:, None]
    x = np.arange(points)[None, :]
    cosine = np.cos(2.0 * math.pi * (j * x % points) / points)
    sine = np.sin(2.0 * math.pi * ((points - j) * x % points) / points)
    rows = np.where(j <= points // 2, cosine, sine) * math.sqrt(2.0 / points)
    return np.where((j == 0) | (j == points // 2), rows * math.sqrt(0.5), rows)


def kinetic_matrix(points):
    basis = real_basis(points)
    return basis.T @ (0.5 * wavenumbers_squared(points)[:, None] * basis)


def split(values):
    high = values.astype(jnp.bfloat16)
    return high, (values - high.astype(jnp.float32)).astype(jnp.bfloat16)


def dot(a, b):
    return jnp.dot(a, b, preferred_element_type=jnp.float32)


def left(matrix_high, matrix_low, values):
    high, low = split(values)
    return dot(jnp.concatenate([matrix_high, matrix_high], 1), jnp.concatenate([high, low], 0)) + dot(matrix_low, high)


def right(values, matrix_high, matrix_low):
    high, low = split(values)
    return dot(jnp.concatenate([high, low], 1), jnp.concatenate([matrix_high, matrix_high], 0)) + dot(high, matrix_low)


def exact(a, b):
    return jnp.dot(a, b, precision=lax.Precision.HIGHEST, preferred_element_type=jnp.float32)


def partner(me, step):
    step = (step * 37) & 63
    y = (me + (step & 48)) & 48
    x = (me + (step & 12)) & 12
    return y | x | ((me ^ step) & 3)


def remote(source, target, send, recv, device):
    pltpu.make_async_remote_copy(
        src_ref=source, dst_ref=target, send_sem=send, recv_sem=recv, device_id=device, device_id_type=MESH
    ).start()


def wait_bytes(part, sem):
    pltpu.make_async_copy(part, part, sem).wait()


def kernel(
    tables_hbm, occupations_ref, psi_hbm, rest_hbm, ionic_hbm, acc, potential_ref,
    tables, high_ref, low_ref, psi, pen, res, back, rest, ionic, part, relay, shares, density, spectrum, lines_in, lines_out, spectrum_back,
    load_sem, small_sem, fwd_send, fwd_recv, bwd_send, bwd_recv, small_send, small_recv,
):
    band, me = lax.axis_index("band"), lax.axis_index("slab")
    points = psi.shape[-1]
    barrier = pltpu.get_barrier_semaphore()

    @pl.loop(1, 64, unroll=7)
    def _(step):
        pl.semaphore_signal(barrier, inc=1, device_id=(band, partner(me, step)), device_id_type=MESH)

    for step in range(1, 4):
        pl.semaphore_signal(barrier, inc=1, device_id=(lax.rem(band + step, 4), me), device_id_type=MESH)

    basis_ref, basis_t_ref = tables.at[0], tables.at[1]
    def load(c):
        for group in range(4):
            o = group * 4 + c
            pltpu.make_async_copy(psi_hbm.at[:, o], psi.at[:, o], load_sem.at[c]).start()

    for c in range(CHUNKS):
        load(c)
    load_rest = pltpu.make_async_copy(rest_hbm, rest, small_sem.at[0])
    load_rest.start()
    load_tables = pltpu.make_async_copy(tables_hbm, tables, small_sem.at[2])
    load_tables.start()
    load_ionic = pltpu.make_async_copy(ionic_hbm, ionic, small_sem.at[1])
    load_ionic.start()
    wait_bytes(pen.at[0], load_sem.at[0])
    pl.semaphore_wait(barrier, 66)

    def field_part(ref, owner, c):
        rows = pl.ds(pl.multiple_of((owner >> 2) * 8, 8), 8)
        return ref.at[:, (owner & 3) * 4 + c, :, rows, :]

    def forward(c):
        @pl.loop(1, 64, unroll=7)
        def _(step):
            other = partner(me, step)
            remote(field_part(psi, other, c), pen.at[c, :, me], fwd_send.at[c], fwd_recv.at[c], (band, other))

        pltpu.make_async_copy(field_part(psi, me, c), pen.at[c, :, me], fwd_recv.at[c]).start()

    def backward(c):
        @pl.loop(1, 64, unroll=7)
        def _(step):
            other = partner(me, step)
            remote(res.at[c, :, other], field_part(back, me, c), bwd_send.at[c], bwd_recv.at[c], (band, other))

        pltpu.make_async_copy(res.at[c, :, me], field_part(back, me, c), bwd_recv.at[c]).start()

    def lines(c):
        wait_bytes(pen.at[c], fwd_recv.at[c])
        source, target = pen.reshape(CHUNKS, 2, 8 * points, points), res.reshape(CHUNKS, 2, 8 * points, points)
        for row in range(8):
            rows = pl.ds(row, points, stride=8)
            values = jnp.concatenate([source[c, 0, rows, :], source[c, 1, rows, :]], 1)
            values = left(high_ref[...], low_ref[...], values)
            target[c, 0, rows, :] = values[:, :points]
            target[c, 1, rows, :] = values[:, points:]

    def planes(c):
        @pl.loop(0, 8)
        def _(i):
            o, x = i // 2 * 4 + c, lax.rem(i, 2)
            real, imag = psi[0, o, x], psi[1, o, x]
            along_y = left(high_ref[...], low_ref[...], jnp.concatenate([real, imag], 1))
            along_z = right(jnp.concatenate([real, imag], 0), high_ref[...], low_ref[...])
            acc[0, o, x] = along_y[:, :points] + along_z[:points]
            acc[1, o, x] = along_y[:, points:] + along_z[points:]

    def finish(c):
        wait_bytes(pen.at[c], bwd_recv.at[c])

        @pl.loop(0, 8)
        def _(i):
            o, x = i // 2 * 4 + c, lax.rem(i, 2)
            potential = potential_ref[x]
            real = acc[0, o, x] + back[0, o, x] + potential * psi[0, o, x]
            imag = acc[1, o, x] + back[1, o, x] + potential * psi[1, o, x]
            acc[0, o, x] = time_step * imag
            acc[1, o, x] = -time_step * real

    after, before, across = lax.rem(band + 1, 4), lax.rem(band + 3, 4), lax.rem(band + 2, 4)

    def rows_of(owner, start, size):
        return pl.ds(pl.multiple_of(owner * 32 + start, 16), size)

    def rows_in(ref, owner, start, size):
        return ref.at[:, rows_of(owner, start, size), :]

    def density_share():
        @pl.loop(0, 8)
        def _(i):
            x, rows = i // 4, pl.ds(pl.multiple_of(lax.rem(i, 4) * 32, 32), 32)
            total = jnp.zeros((32, points), jnp.float32)
            for o in range(16):
                real, imag = psi[0, o, x, rows, :], psi[1, o, x, rows, :]
                total = total + occupations_ref[o] * (real * real + imag * imag)
            part[x, rows, :] = total

        remote(rows_in(part, across, 0, 16), relay.at[0], small_send.at[0], small_recv.at[0], (after, me))
        remote(rows_in(part, across, 16, 16), relay.at[1], small_send.at[0], small_recv.at[0], (before, me))

    def density_relay():
        wait_bytes(relay, small_recv.at[0])
        first, second = rows_of(after, 0, 16), rows_of(before, 16, 16)
        part[:, first, :] = part[:, first, :] + relay[0]
        part[:, second, :] = part[:, second, :] + relay[1]
        remote(rows_in(part, after, 0, 32), shares.at[0], small_send.at[1], small_recv.at[1], (after, me))
        remote(rows_in(part, before, 0, 32), shares.at[1], small_send.at[1], small_recv.at[1], (before, me))

    def density_sum():
        wait_bytes(shares, small_recv.at[1])
        load_rest.wait()
        rows = rows_of(band, 0, 32)
        density[:, rows, :] = rest[:, rows, :] + (part[:, rows, :] + shares[0] + shares[1])
        own = rows_in(density, band, 0, 32)
        remote(own, own, small_send.at[2], small_recv.at[2], (after, me))
        remote(own, own, small_send.at[2], small_recv.at[2], (before, me))

    def density_spread():
        wait_bytes(shares, small_recv.at[2])
        first, second = rows_in(density, before, 0, 16), rows_in(density, after, 16, 16)
        remote(first, first, small_send.at[3], small_recv.at[3], (after, me))
        remote(second, second, small_send.at[3], small_recv.at[3], (before, me))

    def owner_of(block):
        return block * 4 + lax.rem(block, 4)

    block = me // 4
    owns = owner_of(block) == me

    def block_of(ref, i):
        return ref.at[:, pl.ds(pl.multiple_of(i * 8, 8), 8), :]

    def spectrum_send():
        wait_bytes(relay, small_recv.at[3])
        half = exact(density[...].reshape(2 * points, points), basis_t_ref[...])
        both = exact(basis_ref[...], jnp.concatenate([half[:points], half[points:]], 1))
        spectrum[0] = both[:, :points]
        spectrum[1] = both[:, points:]

        @pl.loop(0, 16)
        def _(i):
            i = lax.rem(i + block, 16)
            owner = owner_of(i)

            @pl.when(owner != me)
            def _():
                remote(block_of(spectrum, i), lines_in.at[me], small_send.at[4], small_recv.at[4], (band, owner))

            @pl.when(owner == me)
            def _():
                pltpu.make_async_copy(block_of(spectrum, i), lines_in.at[me], small_recv.at[4]).start()

    def hartree_lines():
        @pl.when(owns)
        def _():
            wait_bytes(lines_in, small_recv.at[4])
            source, target = lines_in.reshape(8 * points, points), lines_out.reshape(8 * points, points)

            def folded(i):
                return jnp.minimum(i, points - i)

            kx = folded(lax.broadcasted_iota(jnp.int32, (points, points), 0))
            kz = folded(lax.broadcasted_iota(jnp.int32, (points, points), 1))
            unit = 4.0 * math.pi * (points * grid_spacing / (2.0 * math.pi)) ** 2

            def green(row):
                ky = folded(block * 8 + row)
                square = kx * kx + kz * kz + ky * ky
                return jnp.where(square > 0, unit / jnp.maximum(square, 1).astype(jnp.float32), 0.0)

            for row in range(0, 8, 2):
                first, second = pl.ds(row, points, stride=8), pl.ds(row + 1, points, stride=8)
                values = exact(basis_ref[...], jnp.concatenate([source[first, :], source[second, :]], 1))
                values = values * jnp.concatenate([green(row), green(row + 1)], 1)
                values = exact(basis_t_ref[...], values)
                target[first, :] = values[:, :points]
                target[second, :] = values[:, points:]

            @pl.loop(1, 64, unroll=7)
            def _(step):
                other = partner(me, step)
                remote(lines_out.at[other], block_of(spectrum_back, block), small_send.at[5], small_recv.at[5], (band, other))

            pltpu.make_async_copy(lines_out.at[me], block_of(spectrum_back, block), small_recv.at[5]).start()

    def potential_sum():
        wait_bytes(spectrum_back, small_recv.at[5])
        half = exact(spectrum_back[...].reshape(2 * points, points), basis_ref[...])
        both = exact(basis_t_ref[...], jnp.concatenate([half[:points], half[points:]], 1))
        load_ionic.wait()
        for x in range(2):
            here = density[x]
            root = jnp.exp(jnp.log(here) * (1.0 / 3.0))
            root = root - (root * root * root - here) / (3.0 * root * root)
            potential_ref[x] = ionic[x] + both[:, x * points : (x + 1) * points] - exchange_factor * root

    forward(0)
    for c in range(1, CHUNKS):
        wait_bytes(pen.at[0], load_sem.at[c])
    load_tables.wait()
    high_ref[...], low_ref[...] = split(tables[2])
    density_share()
    forward(1)
    density_relay()
    planes(0)
    forward(2)
    density_sum()
    planes(1)
    forward(3)
    density_spread()
    planes(2)
    lines(0)
    backward(0)
    spectrum_send()
    lines(1)
    backward(1)
    hartree_lines()
    planes(3)
    lines(2)
    backward(2)
    lines(3)
    backward(3)
    potential_sum()
    finish(0)
    finish(1)
    finish(2)
    finish(3)
    for c in range(CHUNKS):
        wait_bytes(pen.at[c, :, pl.ds(0, 63)], fwd_send.at[c])
        wait_bytes(pen.at[c, :, pl.ds(0, 63)], bwd_send.at[c])
    wait_bytes(relay, small_send.at[0])
    wait_bytes(shares, small_send.at[1])
    wait_bytes(shares, small_send.at[2])
    wait_bytes(relay, small_send.at[3])

    @pl.when(owns)
    def _():
        wait_bytes(lines_in.at[pl.ds(0, 15)], small_send.at[4])
        wait_bytes(lines_in.at[pl.ds(0, 63)], small_send.at[5])

    @pl.when(jnp.logical_not(owns))
    def _():
        wait_bytes(lines_in.at[pl.ds(0, 16)], small_send.at[4])


def pass_on(applied, potential, out_hbm, potential_out_hbm, sems):
    copies = [
        pltpu.make_async_copy(applied.at[p, pl.ds(o, 4)], out_hbm.at[p, pl.ds(o, 4)], sems.at[p * 4 + o // 4])
        for p in range(2)
        for o in range(0, 16, 4)
    ]
    copies.append(pltpu.make_async_copy(potential, potential_out_hbm, sems.at[8]))
    for copy in copies:
        copy.start()
    for copy in copies:
        copy.wait()


def local(orbitals, occupations, rest_density, ionic_potential):
    points = orbitals.shape[3]
    basis = real_basis(points)
    tables = np.stack([basis, basis.T, kinetic_matrix(points)])
    slab_shape = rest_density.shape
    field, slab = pltpu.VMEM(orbitals.shape, jnp.float32), pltpu.VMEM(slab_shape, jnp.float32)
    pencil = pltpu.VMEM((CHUNKS, 2, 64, 2, 8, points), jnp.float32)
    lines = pltpu.VMEM((64, 2, 8, points), jnp.float32)
    dma = pltpu.SemaphoreType.DMA
    in_vmem, anywhere = pl.BlockSpec(memory_space=pltpu.VMEM), pl.BlockSpec(memory_space=pl.ANY)
    applied, potential = pl.pallas_call(
        kernel,
        out_shape=(
            pltpu.VMEM(orbitals.shape, jnp.float32),
            pltpu.VMEM(slab_shape, jnp.float32),
        ),
        in_specs=[anywhere, pl.BlockSpec(memory_space=pltpu.SMEM), anywhere, anywhere, anywhere],
        out_specs=(in_vmem, in_vmem),
        scratch_shapes=[
            pltpu.VMEM(tables.shape, jnp.float32),
            pltpu.VMEM((points, points), jnp.bfloat16), pltpu.VMEM((points, points), jnp.bfloat16), field, pencil, pencil, field, slab, slab, slab,
            pltpu.VMEM((2, 2, 16, points), jnp.float32), pltpu.VMEM((2, 2, 32, points), jnp.float32), slab, slab, lines, lines, slab,
            dma((CHUNKS,)), dma((3,)), dma((CHUNKS,)), dma((CHUNKS,)), dma((CHUNKS,)), dma((CHUNKS,)), dma((6,)), dma((6,)),
        ],
        compiler_params=pltpu.CompilerParams(collective_id=0, has_side_effects=True, vmem_limit_bytes=58 * 2**20),
        cost_estimate=pl.CostEstimate(flops=10**10, bytes_accessed=2**25, transcendentals=0),
    )(
        jnp.asarray(tables, jnp.float32), occupations, orbitals, rest_density, ionic_potential,
    )
    return pl.pallas_call(
        pass_on,
        out_shape=(
            jax.ShapeDtypeStruct(orbitals.shape, jnp.float32),
            jax.ShapeDtypeStruct(slab_shape, jnp.float32),
        ),
        in_specs=[anywhere] * 2,
        out_specs=(anywhere, anywhere),
        scratch_shapes=[dma((9,))],
        compiler_params=pltpu.CompilerParams(vmem_limit_bytes=2**20),
    )(applied, potential)


def solution(mesh):
    return jax.shard_map(
        local,
        mesh=mesh,
        in_specs=(
            P(None, "band", "slab", None, None),
            P("band"),
            P("slab", None, None),
            P("slab", None, None),
        ),
        out_specs=(P(None, "band", "slab", None, None), P("slab", None, None)),
        check_vma=False,
    )
```

```python
import functools
import math

import jax
import jax.numpy as jnp
import numpy as np
from jax import lax
from jax.experimental import pallas as pl
from jax.experimental.pallas import tpu as pltpu
from jax.sharding import PartitionSpec as P

MESH = pl.DeviceIdType.MESH
grid_spacing = 0.4
time_step = 0.01
exchange_factor = (3.0 / math.pi) ** (1.0 / 3.0)
CHUNKS = 4


def wavenumbers_squared(points):
    indices = np.arange(points)
    signed = np.where(indices < points // 2, indices, indices - points)
    return (2.0 * math.pi / (points * grid_spacing) * signed) ** 2


def real_basis(points):
    j = np.arange(points)[:, None]
    x = np.arange(points)[None, :]
    cosine = np.cos(2.0 * math.pi * (j * x % points) / points)
    sine = np.sin(2.0 * math.pi * ((points - j) * x % points) / points)
    rows = np.where(j <= points // 2, cosine, sine) * math.sqrt(2.0 / points)
    return np.where((j == 0) | (j == points // 2), rows * math.sqrt(0.5), rows)


def kinetic_matrix(points):
    basis = real_basis(points)
    return basis.T @ (0.5 * wavenumbers_squared(points)[:, None] * basis)


def split(values):
    high = values.astype(jnp.bfloat16)
    return high, (values - high.astype(jnp.float32)).astype(jnp.bfloat16)


def dot(a, b):
    return jnp.dot(a, b, preferred_element_type=jnp.float32)


def left_split(matrix_high, matrix_low, high, low):
    return dot(jnp.concatenate([matrix_high, matrix_high], 1), jnp.concatenate([high, low], 0)) + dot(matrix_low, high)


def left(matrix_high, matrix_low, values):
    return left_split(matrix_high, matrix_low, *split(values))


def right_split(high, low, matrix_high, matrix_low):
    return dot(jnp.concatenate([high, low], 1), jnp.concatenate([matrix_high, matrix_high], 0)) + dot(high, matrix_low)


def exact(a, b):
    return jnp.dot(a, b, precision=lax.Precision.HIGHEST, preferred_element_type=jnp.float32)


def partner(me, step):
    step = (step * 37) & 63
    y = (me + (step & 48)) & 48
    x = (me + (step & 12)) & 12
    return y | x | ((me ^ step) & 3)


def remote(source, target, send, recv, device):
    pltpu.make_async_remote_copy(
        src_ref=source, dst_ref=target, send_sem=send, recv_sem=recv, device_id=device, device_id_type=MESH
    ).start()


def wait_bytes(part, sem):
    pltpu.make_async_copy(part, part, sem).wait()


def kernel(
    tables_hbm, occupations_ref, psi_hbm, rest_hbm, ionic_hbm, acc, potential_ref,
    tables, high_ref, low_ref, psi, pen, res, back, rest, ionic, part, relay, shares, density, spectrum, lines_in, lines_out, spectrum_back,
    load_sem, small_sem, fwd_send, fwd_recv, bwd_send, bwd_recv, small_send, small_recv,
):
    band, me = lax.axis_index("band"), lax.axis_index("slab")
    points = psi.shape[-1]
    barrier = pltpu.get_barrier_semaphore()

    @pl.loop(1, 64, unroll=7)
    def _(step):
        pl.semaphore_signal(barrier, inc=1, device_id=(band, partner(me, step)), device_id_type=MESH)

    for step in range(1, 4):
        pl.semaphore_signal(barrier, inc=1, device_id=(lax.rem(band + step, 4), me), device_id_type=MESH)

    basis_ref, basis_t_ref = tables.at[0], tables.at[1]
    def load(c):
        for group in range(4):
            o = group * 4 + c
            pltpu.make_async_copy(psi_hbm.at[:, o], psi.at[:, o], load_sem.at[c]).start()

    for c in range(CHUNKS):
        load(c)
    load_rest = pltpu.make_async_copy(rest_hbm, rest, small_sem.at[0])
    load_rest.start()
    load_tables = pltpu.make_async_copy(tables_hbm, tables, small_sem.at[2])
    load_tables.start()
    load_ionic = pltpu.make_async_copy(ionic_hbm, ionic, small_sem.at[1])
    load_ionic.start()
    wait_bytes(pen.at[0], load_sem.at[0])
    pl.semaphore_wait(barrier, 66)

    def field_part(ref, owner, c):
        rows = pl.ds(pl.multiple_of((owner >> 2) * 8, 8), 8)
        return ref.at[:, (owner & 3) * 4 + c, :, rows, :]

    def forward(c):
        @pl.loop(1, 64, unroll=7)
        def _(step):
            other = partner(me, step)
            remote(field_part(psi, other, c), pen.at[c, :, me], fwd_send.at[c], fwd_recv.at[c], (band, other))

        pltpu.make_async_copy(field_part(psi, me, c), pen.at[c, :, me], fwd_recv.at[c]).start()

    def backward(c):
        @pl.loop(1, 64, unroll=7)
        def _(step):
            other = partner(me, step)
            remote(res.at[c, :, other], field_part(back, me, c), bwd_send.at[c], bwd_recv.at[c], (band, other))

        pltpu.make_async_copy(res.at[c, :, me], field_part(back, me, c), bwd_recv.at[c]).start()

    def lines(c):
        wait_bytes(pen.at[c], fwd_recv.at[c])
        source, target = pen.reshape(CHUNKS, 2, 8 * points, points), res.reshape(CHUNKS, 2, 8 * points, points)
        for row in range(8):
            rows = pl.ds(row, points, stride=8)
            values = jnp.concatenate([source[c, 0, rows, :], source[c, 1, rows, :]], 1)
            values = left(high_ref[...], low_ref[...], values)
            target[c, 0, rows, :] = values[:, :points]
            target[c, 1, rows, :] = values[:, points:]

    def planes(c):
        @pl.loop(0, 8)
        def _(i):
            o, x = i // 2 * 4 + c, lax.rem(i, 2)
            real, imag = psi[0, o, x], psi[1, o, x]
            real_high, real_low = split(real)
            imag_high, imag_low = split(imag)
            along_y = left_split(high_ref[...], low_ref[...], jnp.concatenate([real_high, imag_high], 1), jnp.concatenate([real_low, imag_low], 1))
            along_z = right_split(jnp.concatenate([real_high, imag_high], 0), jnp.concatenate([real_low, imag_low], 0), high_ref[...], low_ref[...])
            acc[0, o, x] = along_y[:, :points] + along_z[:points]
            acc[1, o, x] = along_y[:, points:] + along_z[points:]

    def finish(c):
        wait_bytes(pen.at[c], bwd_recv.at[c])

        @pl.loop(0, 8)
        def _(i):
            o, x = i // 2 * 4 + c, lax.rem(i, 2)
            potential = potential_ref[x]
            real = acc[0, o, x] + back[0, o, x] + potential * psi[0, o, x]
            imag = acc[1, o, x] + back[1, o, x] + potential * psi[1, o, x]
            acc[0, o, x] = time_step * imag
            acc[1, o, x] = -time_step * real

    after, before, across = lax.rem(band + 1, 4), lax.rem(band + 3, 4), lax.rem(band + 2, 4)

    def rows_of(owner, start, size):
        return pl.ds(pl.multiple_of(owner * 32 + start, 16), size)

    def rows_in(ref, owner, start, size):
        return ref.at[:, rows_of(owner, start, size), :]

    def density_share():
        @pl.loop(0, 8)
        def _(i):
            x, rows = i // 4, pl.ds(pl.multiple_of(lax.rem(i, 4) * 32, 32), 32)
            total = jnp.zeros((32, points), jnp.float32)
            for o in range(16):
                real, imag = psi[0, o, x, rows, :], psi[1, o, x, rows, :]
                total = total + occupations_ref[o] * (real * real + imag * imag)
            part[x, rows, :] = total

        remote(rows_in(part, across, 0, 16), relay.at[0], small_send.at[0], small_recv.at[0], (after, me))
        remote(rows_in(part, across, 16, 16), relay.at[1], small_send.at[0], small_recv.at[0], (before, me))

    def density_relay():
        wait_bytes(relay, small_recv.at[0])
        first, second = rows_of(after, 0, 16), rows_of(before, 16, 16)
        part[:, first, :] = part[:, first, :] + relay[0]
        part[:, second, :] = part[:, second, :] + relay[1]
        remote(rows_in(part, after, 0, 32), shares.at[0], small_send.at[1], small_recv.at[1], (after, me))
        remote(rows_in(part, before, 0, 32), shares.at[1], small_send.at[1], small_recv.at[1], (before, me))

    def density_sum():
        wait_bytes(shares, small_recv.at[1])
        load_rest.wait()
        rows = rows_of(band, 0, 32)
        density[:, rows, :] = rest[:, rows, :] + (part[:, rows, :] + shares[0] + shares[1])
        own = rows_in(density, band, 0, 32)
        remote(own, own, small_send.at[2], small_recv.at[2], (after, me))
        remote(own, own, small_send.at[2], small_recv.at[2], (before, me))

    def density_spread():
        wait_bytes(shares, small_recv.at[2])
        first, second = rows_in(density, before, 0, 16), rows_in(density, after, 16, 16)
        remote(first, first, small_send.at[3], small_recv.at[3], (after, me))
        remote(second, second, small_send.at[3], small_recv.at[3], (before, me))

    def owner_of(block):
        return block * 4 + lax.rem(block, 4)

    block = me // 4
    owns = owner_of(block) == me

    def block_of(ref, i):
        return ref.at[:, pl.ds(pl.multiple_of(i * 8, 8), 8), :]

    def spectrum_send():
        wait_bytes(relay, small_recv.at[3])
        half = exact(density[...].reshape(2 * points, points), basis_t_ref[...])
        both = exact(basis_ref[...], jnp.concatenate([half[:points], half[points:]], 1))
        spectrum[0] = both[:, :points]
        spectrum[1] = both[:, points:]

        @pl.loop(0, 16)
        def _(i):
            i = lax.rem(i + block, 16)
            owner = owner_of(i)

            @pl.when(owner != me)
            def _():
                remote(block_of(spectrum, i), lines_in.at[me], small_send.at[4], small_recv.at[4], (band, owner))

            @pl.when(owner == me)
            def _():
                pltpu.make_async_copy(block_of(spectrum, i), lines_in.at[me], small_recv.at[4]).start()

    def hartree_lines():
        @pl.when(owns)
        def _():
            wait_bytes(lines_in, small_recv.at[4])
            source, target = lines_in.reshape(8 * points, points), lines_out.reshape(8 * points, points)

            def folded(i):
                return jnp.minimum(i, points - i)

            kx = folded(lax.broadcasted_iota(jnp.int32, (points, points), 0))
            kz = folded(lax.broadcasted_iota(jnp.int32, (points, points), 1))
            unit = 4.0 * math.pi * (points * grid_spacing / (2.0 * math.pi)) ** 2

            def green(row):
                ky = folded(block * 8 + row)
                square = kx * kx + kz * kz + ky * ky
                return jnp.where(square > 0, unit / jnp.maximum(square, 1).astype(jnp.float32), 0.0)

            for row in range(0, 8, 2):
                first, second = pl.ds(row, points, stride=8), pl.ds(row + 1, points, stride=8)
                values = exact(basis_ref[...], jnp.concatenate([source[first, :], source[second, :]], 1))
                values = values * jnp.concatenate([green(row), green(row + 1)], 1)
                values = exact(basis_t_ref[...], values)
                target[first, :] = values[:, :points]
                target[second, :] = values[:, points:]

            @pl.loop(1, 64, unroll=7)
            def _(step):
                other = partner(me, step)
                remote(lines_out.at[other], block_of(spectrum_back, block), small_send.at[5], small_recv.at[5], (band, other))

            pltpu.make_async_copy(lines_out.at[me], block_of(spectrum_back, block), small_recv.at[5]).start()

    def potential_sum():
        wait_bytes(spectrum_back, small_recv.at[5])
        half = exact(spectrum_back[...].reshape(2 * points, points), basis_ref[...])
        both = exact(basis_t_ref[...], jnp.concatenate([half[:points], half[points:]], 1))
        load_ionic.wait()
        for x in range(2):
            here = density[x]
            root = jnp.exp(jnp.log(here) * (1.0 / 3.0))
            root = root - (root * root * root - here) / (3.0 * root * root)
            potential_ref[x] = ionic[x] + both[:, x * points : (x + 1) * points] - exchange_factor * root

    forward(0)
    for c in range(1, CHUNKS):
        wait_bytes(pen.at[0], load_sem.at[c])
    load_tables.wait()
    high_ref[...], low_ref[...] = split(tables[2])
    density_share()
    forward(1)
    density_relay()
    planes(0)
    forward(2)
    density_sum()
    planes(1)
    forward(3)
    density_spread()
    planes(2)
    lines(0)
    backward(0)
    spectrum_send()
    lines(1)
    backward(1)
    hartree_lines()
    planes(3)
    lines(2)
    backward(2)
    lines(3)
    backward(3)
    potential_sum()
    finish(0)
    finish(1)
    finish(2)
    finish(3)
    for c in range(CHUNKS):
        wait_bytes(pen.at[c, :, pl.ds(0, 63)], fwd_send.at[c])
        wait_bytes(pen.at[c, :, pl.ds(0, 63)], bwd_send.at[c])
    wait_bytes(relay, small_send.at[0])
    wait_bytes(shares, small_send.at[1])
    wait_bytes(shares, small_send.at[2])
    wait_bytes(relay, small_send.at[3])

    @pl.when(owns)
    def _():
        wait_bytes(lines_in.at[pl.ds(0, 15)], small_send.at[4])
        wait_bytes(lines_in.at[pl.ds(0, 63)], small_send.at[5])

    @pl.when(jnp.logical_not(owns))
    def _():
        wait_bytes(lines_in.at[pl.ds(0, 16)], small_send.at[4])


def pass_on(applied, potential, out_hbm, potential_out_hbm, sems):
    copies = [
        pltpu.make_async_copy(applied.at[p, pl.ds(o, 4)], out_hbm.at[p, pl.ds(o, 4)], sems.at[p * 4 + o // 4])
        for p in range(2)
        for o in range(0, 16, 4)
    ]
    copies.append(pltpu.make_async_copy(potential, potential_out_hbm, sems.at[8]))
    for copy in copies:
        copy.start()
    for copy in copies:
        copy.wait()


def local(orbitals, occupations, rest_density, ionic_potential):
    points = orbitals.shape[3]
    basis = real_basis(points)
    tables = np.stack([basis, basis.T, kinetic_matrix(points)])
    slab_shape = rest_density.shape
    field, slab = pltpu.VMEM(orbitals.shape, jnp.float32), pltpu.VMEM(slab_shape, jnp.float32)
    pencil = pltpu.VMEM((CHUNKS, 2, 64, 2, 8, points), jnp.float32)
    lines = pltpu.VMEM((64, 2, 8, points), jnp.float32)
    dma = pltpu.SemaphoreType.DMA
    in_vmem, anywhere = pl.BlockSpec(memory_space=pltpu.VMEM), pl.BlockSpec(memory_space=pl.ANY)
    applied, potential = pl.pallas_call(
        kernel,
        out_shape=(
            pltpu.VMEM(orbitals.shape, jnp.float32),
            pltpu.VMEM(slab_shape, jnp.float32),
        ),
        in_specs=[anywhere, pl.BlockSpec(memory_space=pltpu.SMEM), anywhere, anywhere, anywhere],
        out_specs=(in_vmem, in_vmem),
        scratch_shapes=[
            pltpu.VMEM(tables.shape, jnp.float32),
            pltpu.VMEM((points, points), jnp.bfloat16), pltpu.VMEM((points, points), jnp.bfloat16), field, pencil, pencil, field, slab, slab, slab,
            pltpu.VMEM((2, 2, 16, points), jnp.float32), pltpu.VMEM((2, 2, 32, points), jnp.float32), slab, slab, lines, lines, slab,
            dma((CHUNKS,)), dma((3,)), dma((CHUNKS,)), dma((CHUNKS,)), dma((CHUNKS,)), dma((CHUNKS,)), dma((6,)), dma((6,)),
        ],
        compiler_params=pltpu.CompilerParams(collective_id=0, has_side_effects=True, vmem_limit_bytes=58 * 2**20),
        cost_estimate=pl.CostEstimate(flops=10**10, bytes_accessed=2**25, transcendentals=0),
    )(
        jnp.asarray(tables, jnp.float32), occupations, orbitals, rest_density, ionic_potential,
    )
    return pl.pallas_call(
        pass_on,
        out_shape=(
            jax.ShapeDtypeStruct(orbitals.shape, jnp.float32),
            jax.ShapeDtypeStruct(slab_shape, jnp.float32),
        ),
        in_specs=[anywhere] * 2,
        out_specs=(anywhere, anywhere),
        scratch_shapes=[dma((9,))],
        compiler_params=pltpu.CompilerParams(vmem_limit_bytes=2**20),
    )(applied, potential)


def solution(mesh):
    return jax.shard_map(
        local,
        mesh=mesh,
        in_specs=(
            P(None, "band", "slab", None, None),
            P("band"),
            P("slab", None, None),
            P("slab", None, None),
        ),
        out_specs=(P(None, "band", "slab", None, None), P("slab", None, None)),
        check_vma=False,
    )
```
